128 devices in a mesh: row: 8 (over y, core), col: 16 (over x, z).
Axes of the slice: x: 4, y: 4, z: 4, core: 2. Of those that a mesh axis runs over, the one named last changes fastest.
Arguments:
- tokens: bfloat16 [1920, 8192], P('col', 'row'), may hold values from -6 to 6
- cotangent: bfloat16 [1920, 8192], P('col', 'row'), may hold values from -6 to 6
- gate_weight: bfloat16 [8192, 14336], P('row', 'col'), may hold values from -0.0625 to 0.0625
- up_weight: bfloat16 [8192, 14336], P('row', 'col'), may hold values from -0.0625 to 0.0625
- down_weight: bfloat16 [14336, 8192], P('col', 'row'), may hold values from -0.046875 to 0.046875
Outputs:
- grad_input: bfloat16 [1920, 8192], P('col', 'row')
- grad_gate: float32 [8192, 14336], P('row', 'col')
- grad_up: float32 [8192, 14336], P('row', 'col')
- grad_down: float32 [14336, 8192], P('col', 'row')
The draws below stay inside these ranges and needn't reach their ends.
All inputs are finite; a program needn't handle non-finite values.
Results may differ from the reference program's by a relative error of at most 0.03.
Values may be sent and summed in bfloat16 or wider, within the bound.
No kernel may reach another device: no remote copies, remote signals or barrier semaphores. Data moves between devices by JAX's collectives and lax.ppermute only.
A program may use at most 128 MiB of HBM per device.

```python
import jax
import jax.numpy as jnp
from jax import lax

D = 8192
FF = 14336
TOKENS = 1920
N_ROW = 8


def level_of(own_key, dims, pieces, low, top_value):
    loudness = 1.0
    for dim, shards_of in pieces:
        steps = jax.random.uniform(jax.random.fold_in(jax.random.fold_in(own_key, 6), dim), (shards_of,), jnp.float32, low / len(pieces), top_value / len(pieces))
        loudness = loudness * jnp.repeat(jnp.exp(steps), dims[dim] // shards_of).reshape((-1,) + (1,) * (len(dims) - 1 - dim))
    return loudness


def gaussian(rng, dims, deviation, most, pieces=(), dtype=jnp.bfloat16):
    gain = level_of(rng, dims, pieces, -0.22, 0.18) if pieces else 1.0
    array = jax.random.normal(rng, dims, jnp.float32) * deviation * gain
    return jnp.minimum(jnp.maximum(array, -most), most).astype(dtype)


def setup_inputs(seed: int = 0) -> dict:
    arg_keys = jax.random.split(jax.random.key(seed), 6)
    return {
        "tokens": gaussian(arg_keys[0], (TOKENS, D), 1.0, 6.0, ((0, 16), (1, 8))),
        "cotangent": gaussian(arg_keys[1], (TOKENS, D), 1.0, 6.0, ((0, 16), (1, 8))),
        "gate_weight": gaussian(arg_keys[2], (D, FF), D ** -0.5, 0.0625, ((0, 8), (1, 16))),
        "up_weight": gaussian(arg_keys[3], (D, FF), D ** -0.5, 0.0625, ((0, 8), (1, 16))),
        "down_weight": gaussian(arg_keys[4], (FF, D), FF ** -0.5, 0.046875, ((0, 16), (1, 8))),
    }


def rounded(value):
    return lax.optimization_barrier(value.astype(jnp.bfloat16)).astype(jnp.float32)


def reference(tokens, cotangent, gate_weight, up_weight, down_weight):
    block_width = D // N_ROW
    gate_sum = jnp.zeros((TOKENS, FF), jnp.float32)
    up_sum = jnp.zeros((TOKENS, FF), jnp.float32)
    hidden_grad = jnp.zeros((TOKENS, FF), jnp.float32)
    for block_index in range(N_ROW):
        first = block_index * block_width
        rows_in = tokens[:, first:first + block_width]
        rows_cot = cotangent[:, first:first + block_width]
        gate_sum = gate_sum + rounded(jnp.dot(rows_in, gate_weight[first:first + block_width, :], preferred_element_type=jnp.float32))
        up_sum = up_sum + rounded(jnp.dot(rows_in, up_weight[first:first + block_width, :], preferred_element_type=jnp.float32))
        hidden_grad = hidden_grad + rounded(jnp.dot(rows_cot, down_weight[:, first:first + block_width].T, preferred_element_type=jnp.float32))
    sigmoid_gate = jax.nn.sigmoid(gate_sum)
    silu_gate = gate_sum * sigmoid_gate
    hidden = (silu_gate * up_sum).astype(jnp.bfloat16)
    gate_grad = (hidden_grad * up_sum * sigmoid_gate * (1.0 + gate_sum * (1.0 - sigmoid_gate))).astype(jnp.bfloat16)
    up_grad = (hidden_grad * silu_gate).astype(jnp.bfloat16)
    grad_down = jnp.dot(hidden.T, cotangent, preferred_element_type=jnp.float32)
    grad_gate = jnp.dot(tokens.T, gate_grad, preferred_element_type=jnp.float32)
    grad_up = jnp.dot(tokens.T, up_grad, preferred_element_type=jnp.float32)
    grad_input = jnp.dot(gate_grad, gate_weight.T, preferred_element_type=jnp.float32)
    grad_input = grad_input + jnp.dot(up_grad, up_weight.T, preferred_element_type=jnp.float32)
    return grad_input.astype(jnp.bfloat16), grad_gate, grad_up, grad_down
```

```python
import jax
import jax.numpy as jnp
from jax import lax
from jax.sharding import PartitionSpec as P

BF16 = jnp.bfloat16
F32 = jnp.float32
STRIPES = ((0, 56), (56, 120))
AXES = ("row", "col")


def device(y, core, x, z):
    return (((y % 4) * 2 + core) * 4 + x % 4) * 4 + z % 4


def pairs(move):
    return [
        (device(y, c, x, z), device(*move(y, c, x, z)))
        for y in range(4)
        for c in range(2)
        for x in range(4)
        for z in range(4)
    ]


def sign(c):
    return 1 - 2 * c


ALONG_Y = pairs(lambda y, c, x, z: (y + sign(c), c, x, z))
ALONG_X = pairs(lambda y, c, x, z: (y, c, x + sign(c), z))
ALONG_Z = pairs(lambda y, c, x, z: (y, c, x, z + sign(c)))
TO_TWIN = pairs(lambda y, c, x, z: (y, 1 - c, x, z))


def first_axis(k):
    return pairs(lambda y, c, x, z: (y, c, x, z + k) if c == 0 else (y, c, x + k, z))


def second_axis(k):
    return pairs(lambda y, c, x, z: (y, c, x + k, z) if c == 0 else (y, c, x, z + k))


def send(value, perm):
    return lax.ppermute(value, AXES, perm)


def pick(array, index, axis):
    return lax.dynamic_index_in_dim(array, index, axis, keepdims=False)


def put(array, value, index, axis):
    return lax.dynamic_update_index_in_dim(array, value, index, axis)


def gather_ring(value, perm, place, step, axis_shape, axis=0):
    shape = value.shape[:axis] + (4,) + value.shape[axis:]
    whole = put(jnp.zeros(shape, value.dtype), value, place, axis)
    for t in range(1, 4):
        value = send(value, perm)
        whole = put(whole, value, (place - step * t) % 4, axis)
    return whole


def contract_rows(left, right):
    return lax.dot_general(
        left, right, (((0,), (0,)), ((), ())), preferred_element_type=F32
    )


def contract_cols(left, right):
    return lax.dot_general(
        left, right, (((1,), (1,)), ((), ())), preferred_element_type=F32
    )


def local_grads(gate_sum, up_sum, hidden_grad):
    s = jax.nn.sigmoid(gate_sum)
    silu = gate_sum * s
    hidden = (silu * up_sum).astype(BF16)
    gate_grad = (hidden_grad * up_sum * s * (1.0 + gate_sum * (1.0 - s))).astype(BF16)
    up_grad = (hidden_grad * silu).astype(BF16)
    return hidden, gate_grad, up_grad


def local(tokens, cotangent, gate_weight, up_weight, down_weight):
    row, col = lax.axis_index("row"), lax.axis_index("col")
    y, c, x, z = row // 2, row % 2, col // 4, col % 4
    step = 1 - 2 * c
    width = tokens.shape[1]
    units = gate_weight.shape[1]

    def panels(first, last):
        n = last - first
        tk, ct = tokens[first:last], cotangent[first:last]
        zline = gather_ring(tk, ALONG_Z, z, step, None)
        xline = gather_ring(ct, ALONG_X, x, step, None)
        whole_in = gather_ring(zline, ALONG_X, x, step, None)
        whole_cot = gather_ring(xline, ALONG_Z, z, step, None, axis=1)
        return (
            whole_in.reshape(16 * n, width),
            whole_cot.reshape(16 * n, width),
        )

    def reduce_row(panel_in, panel_cot):
        parts = [
            jnp.dot(panel_in, gate_weight, preferred_element_type=F32).astype(BF16),
            jnp.dot(panel_in, up_weight, preferred_element_type=F32).astype(BF16),
            contract_cols(panel_cot, down_weight).astype(BF16),
        ]
        share = parts[0].shape[0] // 8
        parts = [p.reshape(2, 4, share, units) for p in parts]
        other = send(jnp.stack([pick(p, 1 - c, 0) for p in parts]), TO_TWIN)
        half = jnp.stack([pick(p, c, 0) for p in parts]).astype(F32) + other.astype(F32)
        half = half.astype(BF16)
        total = pick(half, (y - step) % 4, 1)
        for t in range(1, 4):
            total = send(total, ALONG_Y).astype(F32) + pick(half, (y - step * (t + 1)) % 4, 1).astype(F32)
            if t < 3:
                total = total.astype(BF16)
        return total[0], total[1], total[2]

    def gather_row(value):
        k = value.shape[0]
        half = gather_ring(value, ALONG_Y, y, step, None, axis=1)
        other = send(half, TO_TWIN)
        whole = jnp.zeros((k, 2) + half.shape[1:], BF16)
        whole = put(whole, half, c, 1)
        whole = put(whole, other, 1 - c, 1)
        return whole.reshape(k, -1, units)

    def scatter_col(value, n):
        value = value.reshape(4, 4, n, width)
        value = jnp.where(c == 0, value.transpose(1, 0, 2, 3), value)
        a, b = jnp.where(c == 0, z, x), jnp.where(c == 0, x, z)
        halves = []
        for d, part in ((1, value[..., : width // 2]), (-1, value[..., width // 2 :])):
            total = pick(part, (a - d) % 4, 0)
            for t in range(1, 4):
                total = send(total, first_axis(d)).astype(F32) + pick(
                    part, (a - d * (t + 1)) % 4, 0
                ).astype(F32)
                if t < 3:
                    total = total.astype(BF16)
            halves.append(total)
        line = jnp.concatenate(halves, axis=-1)
        total = pick(line, b, 0)
        rounded = line.astype(BF16)
        for k in range(1, 4):
            total = total + send(pick(rounded, (b + k) % 4, 0), second_axis(k)).astype(F32)
        return total.astype(BF16)

    gathered = [panels(*s) for s in STRIPES]
    grads = [local_grads(*reduce_row(*g)) for g in gathered]
    panel_in = jnp.concatenate([g[0] for g in gathered])
    panel_cot = jnp.concatenate([g[1] for g in gathered])
    gate_up = [gather_row(jnp.stack([gg, ug])) for _, gg, ug in grads]
    grad_input = []
    for (first, last), gu in zip(STRIPES, gate_up):
        whole = contract_cols(gu[0], gate_weight) + contract_cols(gu[1], up_weight)
        grad_input.append(scatter_col(whole.astype(BF16), last - first))
    grad_input = jnp.concatenate(grad_input)
    grad_gate = contract_rows(panel_in, jnp.concatenate([gu[0] for gu in gate_up]))
    grad_up = contract_rows(panel_in, jnp.concatenate([gu[1] for gu in gate_up]))
    hidden = [gather_row(h[None])[0] for h, _, _ in grads]
    grad_down = contract_rows(jnp.concatenate(hidden), panel_cot)
    return (grad_input, grad_gate, grad_up, grad_down)


def solution(mesh):
    return jax.shard_map(
        local,
        mesh=mesh,
        in_specs=(
            P("col", "row"),
            P("col", "row"),
            P("row", "col"),
            P("row", "col"),
            P("col", "row"),
        ),
        out_specs=(P("col", "row"), P("row", "col"), P("row", "col"), P("col", "row")),
        check_vma=False,
    )
```

```python
import functools

import jax
import jax.numpy as jnp
from jax import lax
from jax.experimental import pallas as pl
from jax.experimental.pallas import tpu as pltpu
from jax.sharding import PartitionSpec as P

BF16 = jnp.bfloat16
F32 = jnp.float32
SPLIT = 64
AXES = ("row", "col")
VMEM_LIMIT = 16 * 2**20


def device(y, core, x, z):
    return (((y % 4) * 2 + core) * 4 + x % 4) * 4 + z % 4


def pairs(move):
    return [
        (device(y, c, x, z), device(*move(y, c, x, z)))
        for y in range(4)
        for c in range(2)
        for x in range(4)
        for z in range(4)
    ]


def sign(c):
    return 1 - 2 * c


ALONG_X = pairs(lambda y, c, x, z: (y, c, x + sign(c), z))
ALONG_Y = pairs(lambda y, c, x, z: (y + sign(c), c, x, z))
ALONG_Z = pairs(lambda y, c, x, z: (y, c, x, z + sign(c)))
TO_TWIN = pairs(lambda y, c, x, z: (y, 1 - c, x, z))


def first_axis(k):
    return pairs(lambda y, c, x, z: (y, c, x, z + k) if c == 0 else (y, c, x + k, z))


def second_axis(k):
    return pairs(lambda y, c, x, z: (y, c, x + k, z) if c == 0 else (y, c, x, z + k))


def send(value, perm):
    return lax.ppermute(value, AXES, perm)


class Clock:
    def __init__(self, start):
        self.now = start

    def gate(self, values):
        out = lax.optimization_barrier((self.now,) + tuple(values))
        self.now = out[0]
        return list(out[1:])

    def arrive(self, *values):
        values = self.gate(values)
        self.now = self.now + 1.0
        return self.gate(values)

    def run(self, call, *values):
        out = call(*self.gate(values))
        return self.gate(out) if isinstance(out, (list, tuple)) else self.gate([out])[0]


def contract_rows(left, right):
    return lax.dot_general(
        left, right, (((0,), (0,)), ((), ())), preferred_element_type=F32
    )


def contract_cols(left, right):
    return lax.dot_general(
        left, right, (((1,), (1,)), ((), ())), preferred_element_type=F32
    )


def local_call(kernel, out_shapes, place, *operands):
    shapes = [jax.ShapeDtypeStruct(s, BF16) for s in out_shapes]
    return pl.pallas_call(
        kernel,
        out_shape=shapes,
        in_specs=[pl.BlockSpec(memory_space=pltpu.SMEM)]
        + [pl.BlockSpec(memory_space=pltpu.VMEM)] * len(operands),
        out_specs=[pl.BlockSpec(memory_space=pltpu.VMEM)] * len(shapes),
        compiler_params=pltpu.CompilerParams(vmem_limit_bytes=VMEM_LIMIT),
        cost_estimate=pl.CostEstimate(flops=1, bytes_accessed=1, transcendentals=0),
    )(place, *operands)


def position(y, c, u, t):
    step = 1 - 2 * c
    twin = jnp.where(t // 2 == c, 0, 1)
    slot = ((y - u) * step * (1 - 2 * twin) + 16) % 4
    return twin * 8 + slot * 2 + t % 2


def stage_kernel(place, *refs):
    count = len(refs) // 2
    for i in range(count):
        refs[count + i][...] = refs[i][...]


def panels_kernel(first, n, place, *refs):
    y, c = place[0], place[1]
    step = 1 - 2 * c
    blocks, (panel_in, panel_cot) = refs[:32], refs[32:]
    rows = pl.ds(first, n)
    for m in range(4):
        for k in range(4):
            far, near = (step * k + 4) % 4, (step * m + 4) % 4
            panel_in[position(y, c, far, near)] = blocks[4 * m + k][rows]
            panel_cot[position(y, c, near, far)] = blocks[16 + 4 * m + k][rows]


def halves_kernel(place, *refs):
    own, twin, first, rest = refs[:3], refs[3:6], refs[6], refs[7]
    rows = first.shape[1]
    for j in range(4):
        for i in range(3):
            part = pl.ds(j * rows, rows)
            total = (own[i][part].astype(F32) + twin[i][part].astype(F32)).astype(BF16)
            if j == 1:
                first[i] = total
            else:
                rest[(j + 2) % 4, i] = total


def add_kernel(j, place, received, rest, total):
    total[...] = (received[...].astype(F32) + rest[j].astype(F32)).astype(BF16)


def grads_kernel(place, received, rest, gate_up, hidden):
    gate_sum = received[0].astype(F32) + rest[2, 0].astype(F32)
    up_sum = received[1].astype(F32) + rest[2, 1].astype(F32)
    hidden_grad = received[2].astype(F32) + rest[2, 2].astype(F32)
    s = 1.0 / (1.0 + jnp.exp(-gate_sum))
    silu = gate_sum * s
    hidden[...] = (silu * up_sum).astype(BF16)
    gate_up[0] = (hidden_grad * up_sum * s * (1.0 + gate_sum * (1.0 - s))).astype(BF16)
    gate_up[1] = (hidden_grad * silu).astype(BF16)


def pair_kernel(place, *refs):
    blocks, (gate, up) = refs[:8], refs[8:]
    rows = blocks[0].shape[1]
    for j in range(8):
        gate[pl.ds(j * rows, rows)] = blocks[j][0]
        up[pl.ds(j * rows, rows)] = blocks[j][1]


def single_kernel(place, *refs):
    blocks, whole = refs[:8], refs[8]
    rows = blocks[0].shape[0]
    for j in range(8):
        whole[pl.ds(j * rows, rows)] = blocks[j][...]


def by_target_kernel(place, part, mine, left, right, far_up, far_down):
    y, c = place[0], place[1]
    mid = part.shape[-1] // 2
    for a in range(4):
        for b in range(4):
            u, t = jnp.where(c == 0, b, a), jnp.where(c == 0, a, b)
            block = part[position(y, c, u, t)]
            if a == 2:
                far_up[b] = block[:, :mid]
                far_down[b] = block[:, mid:]
            else:
                (mine, left, None, right)[a][b] = block


def relay_kernel(place, left, right, up, down, to_left, to_right):
    mid = left.shape[-1] // 2
    to_left[:, :, :mid] = left[:, :, :mid]
    to_left[:, :, mid:] = (left[:, :, mid:].astype(F32) + down[...].astype(F32)).astype(BF16)
    to_right[:, :, :mid] = (right[:, :, :mid].astype(F32) + up[...].astype(F32)).astype(BF16)
    to_right[:, :, mid:] = right[:, :, mid:]


def line_kernel(place, mine, from_left, from_right, own, *others):
    for k in range(4):
        total = mine[k].astype(F32) + from_left[k].astype(F32) + from_right[k].astype(F32)
        if k == 0:
            own[...] = total.astype(BF16)
        else:
            others[k - 1][...] = total.astype(BF16)


def sum_kernel(place, a0, b0, c0, d0, a1, b1, c1, d1, out):
    rows = a0.shape[0]
    for parts, at in (((a0, b0, c0, d0), slice(0, rows)), ((a1, b1, c1, d1), slice(rows, None))):
        total = parts[0][...].astype(F32)
        for p in parts[1:]:
            total = total + p[...].astype(F32)
        out[at] = total.astype(BF16)


def local(tokens, cotangent, gate_weight, up_weight, down_weight):
    row, col = lax.axis_index("row"), lax.axis_index("col")
    place = jnp.stack([row // 2, row % 2]).astype(jnp.int32)
    length, width = tokens.shape
    units = gate_weight.shape[1]
    mid = width // 2
    sizes = (SPLIT, length - SPLIT)

    n0, n1 = sizes
    clock = Clock(jnp.zeros((8, 128), F32))
    arrive, run = clock.arrive, clock.run

    def call(kernel, shapes):
        return lambda *values: local_call(kernel, shapes, place, *values)

    def first(pair):
        return [send(pair[0], ALONG_Z), send(pair[1], ALONG_X)]

    def second(pair):
        return [send(pair[0], ALONG_X), send(pair[1], ALONG_Z)]

    def up_y(value):
        return send(value, ALONG_Y)

    def twin(value):
        return send(value, TO_TWIN)

    far = [[[tokens, cotangent]], [], [], []]
    p = first(far[0][0])
    s0 = second(far[0][0])
    far[1].append(arrive(*p))
    p = first(far[1][0])
    s1 = second(far[1][0])
    weights = [gate_weight, up_weight, down_weight]
    staged = run(
        call(stage_kernel, [w.shape for w in weights + far[0][0]]), *weights, *far[0][0]
    )
    gate_weight, up_weight, down_weight = staged[:3]
    far[0][0] = staged[3:]
    far[0].append(arrive(*s0))
    s0 = second(far[0][1])
    far[2].append(arrive(*p))
    p = first(far[2][0])
    s2 = second(far[2][0])
    far[1].append(arrive(*s1))
    s1 = second(far[1][1])
    far[0].append(arrive(*s0))
    s0 = second(far[0][2])
    far[3].append(arrive(*p))
    s3 = second(far[3][0])
    far[2].append(arrive(*s2))
    s2 = second(far[2][1])
    far[1].append(arrive(*s1))
    s1 = second(far[1][2])
    far[0].append(s0)
    far[3].append(arrive(*s3))
    s3 = second(far[3][1])
    far[2].append(arrive(*s2))
    s2 = second(far[2][2])
    far[1].append(s1)
    far[3].append(arrive(*s3))
    s3 = second(far[3][2])
    far[2].append(s2)
    far[3].append(s3)
    blocks = [far[m][k][i] for i in range(2) for m in range(4) for k in range(4)]

    def panels(start, n, blocks):
        kernel = functools.partial(panels_kernel, start, n)
        both = run(call(kernel, [(16, n, width)] * 2), *blocks)
        return [p.reshape(16 * n, width) for p in both]

    def partials(panel_in, panel_cot):
        gate = run(lambda a, b: jnp.dot(a, b, preferred_element_type=F32).astype(BF16), panel_in, gate_weight)
        up = run(lambda a, b: jnp.dot(a, b, preferred_element_type=F32).astype(BF16), panel_in, up_weight)
        down = run(lambda a, b: contract_cols(a, b).astype(BF16), panel_cot, down_weight)
        return [gate, up, down]

    def halves(n, own, theirs):
        shape = (3, 2 * n, units)
        return run(call(halves_kernel, [shape, (3,) + shape]), *own, *theirs)

    def add(j, received, rest):
        kernel = functools.partial(add_kernel, j)
        return run(call(kernel, [received.shape]), received, rest)[0]

    def grads(n, received, rest):
        return run(call(grads_kernel, [(2, 2 * n, units), (2 * n, units)]), received, rest)

    def pair(n, blocks, twins):
        return run(call(pair_kernel, [(16 * n, units)] * 2), *blocks, *twins)

    def single(n, blocks, twins):
        return run(call(single_kernel, [(16 * n, units)]), *blocks, *twins)[0]

    def to_input(gate, up):
        return run(
            lambda a, b, c, d: (contract_cols(a, b) + contract_cols(c, d)).astype(BF16),
            gate, gate_weight, up, up_weight,
        )

    def arrange(part, n):
        wide, slim = (4, n, width), (4, n, mid)
        part = part.reshape(16, n, width)
        return run(call(by_target_kernel, [wide, wide, wide, slim, slim]), part)

    def relay(n, parts, up, down):
        _, left, right, _, _ = parts
        left, right = run(call(relay_kernel, [(4, n, width)] * 2), left, right, up, down)
        return send(right, first_axis(1)), send(left, first_axis(-1))

    def line(n, parts, from_left, from_right):
        total = run(call(line_kernel, [(n, width)] * 4), parts[0], from_left, from_right)
        return [total[0]] + [send(total[k], second_axis(-k)) for k in (1, 2, 3)]

    def far_ends(parts):
        return send(parts[3], first_axis(1)), send(parts[4], first_axis(-1))

    in0, cot0 = panels(0, n0, blocks)
    theirs0 = [twin(v) for v in partials(in0[8 * n0 :], cot0[8 * n0 :])]
    in1, cot1 = panels(n0, n1, blocks)
    theirs1 = [twin(v) for v in partials(in1[8 * n1 :], cot1[8 * n1 :])]
    own0 = partials(in0[: 8 * n0], cot0[: 8 * n0])
    first0, rest0 = halves(n0, own0, theirs0)
    r0 = up_y(first0)
    own1 = partials(in1[: 8 * n1], cot1[: 8 * n1])
    first1, rest1 = halves(n1, own1, theirs1)
    r1 = up_y(first1)
    r0 = up_y(add(0, r0, rest0))
    r1 = up_y(add(0, r1, rest1))
    r0 = up_y(add(1, r0, rest0))
    r1 = up_y(add(1, r1, rest1))
    gu0, hid0 = grads(n0, r0, rest0)
    g0, g0_twin = [gu0], [twin(gu0)]
    g = up_y(gu0)
    gu1, hid1 = grads(n1, r1, rest1)
    g1, g1_twin = [gu1], [twin(gu1)]
    q = up_y(gu1)
    for hop in range(3):
        g0 += arrive(g)
        if hop < 2:
            g = up_y(g0[-1])
        g0_twin.append(twin(g0[-1]))
        g1 += arrive(q)
        if hop < 2:
            q = up_y(g1[-1])
        g1_twin.append(twin(g1[-1]))
    h0, h1, h0_twin, h1_twin = [hid0], [hid1], [twin(hid0)], [twin(hid1)]
    h, k = [up_y(v) for v in clock.gate([hid0, hid1])]

    def pass_on(more):
        nonlocal h, k
        h0.extend(arrive(h))
        if more:
            h = up_y(h0[-1])
        h0_twin.append(twin(h0[-1]))
        h1.extend(arrive(k))
        if more:
            k = up_y(h1[-1])
        h1_twin.append(twin(h1[-1]))

    gate0, up0 = pair(n0, g0, g0_twin)
    parts0 = arrange(to_input(gate0, up0), n0)
    ends0 = far_ends(parts0)
    pass_on(True)
    gate1, up1 = pair(n1, g1, g1_twin)
    parts1 = arrange(to_input(gate1, up1), n1)
    ends1 = far_ends(parts1)
    sides0 = relay(n0, parts0, *ends0)
    pass_on(True)
    sides1 = relay(n1, parts1, *ends1)
    grad_gate = run(contract_rows, in0, gate0)
    line0 = line(n0, parts0, *sides0)
    pass_on(False)
    grad_up = run(contract_rows, in0, up0)
    line1 = line(n1, parts1, *sides1)

    def accumulate(total, a, b):
        return run(lambda t, a, b: t + contract_rows(a, b), total, a, b)

    grad_gate = accumulate(grad_gate, in1, gate1)
    grad_up = accumulate(grad_up, in1, up1)
    grad_down = run(contract_rows, single(n0, h0, h0_twin), cot0)
    grad_down = accumulate(grad_down, single(n1, h1, h1_twin), cot1)
    grad_input = run(call(sum_kernel, [tokens.shape]), *line0, *line1)[0]
    return (grad_input, grad_gate, grad_up, grad_down)


def solution(mesh):
    return jax.shard_map(
        local,
        mesh=mesh,
        in_specs=(
            P("col", "row"),
            P("col", "row"),
            P("row", "col"),
            P("row", "col"),
            P("col", "row"),
        ),
        out_specs=(P("col", "row"), P("row", "col"), P("row", "col"), P("col", "row")),
        check_vma=False,
    )
```

```python
import functools

import jax
import jax.numpy as jnp
from jax import lax
from jax.experimental import pallas as pl
from jax.experimental.pallas import tpu as pltpu
from jax.sharding import PartitionSpec as P

BF16 = jnp.bfloat16
F32 = jnp.float32
GATE_UP_PIECES = 4
BACK_PIECES = 4
SPLIT = 64
AXES = ("row", "col")
VMEM_LIMIT = 24 * 2**20


def device(y, core, x, z):
    return (((y % 4) * 2 + core) * 4 + x % 4) * 4 + z % 4


def pairs(move):
    return [
        (device(y, c, x, z), device(*move(y, c, x, z)))
        for y in range(4)
        for c in range(2)
        for x in range(4)
        for z in range(4)
    ]


def sign(c):
    return 1 - 2 * c


ALONG_X = pairs(lambda y, c, x, z: (y, c, x + sign(c), z))
ALONG_Y = pairs(lambda y, c, x, z: (y + sign(c), c, x, z))
ALONG_Z = pairs(lambda y, c, x, z: (y, c, x, z + sign(c)))
TO_TWIN = pairs(lambda y, c, x, z: (y, 1 - c, x, z))


def first_axis(k):
    return pairs(lambda y, c, x, z: (y, c, x, z + k) if c == 0 else (y, c, x + k, z))


def second_axis(k):
    return pairs(lambda y, c, x, z: (y, c, x + k, z) if c == 0 else (y, c, x, z + k))


def send(value, perm):
    return lax.ppermute(value, AXES, perm)


def contract_rows(left, right):
    return lax.dot_general(
        left, right, (((0,), (0,)), ((), ())), preferred_element_type=F32
    )


def contract_cols(left, right):
    return lax.dot_general(
        left, right, (((1,), (1,)), ((), ())), preferred_element_type=F32
    )


def local_call(kernel, out_shapes, place, operands, earlier):
    count = len(operands)

    def ordered(place_ref, *refs):
        kernel(place_ref, *refs[:count], *refs[count + len(earlier) :])

    shapes = [s if hasattr(s, "dtype") else jax.ShapeDtypeStruct(s, BF16) for s in out_shapes]
    return pl.pallas_call(
        ordered,
        out_shape=shapes,
        in_specs=[pl.BlockSpec(memory_space=pltpu.SMEM)]
        + [pl.BlockSpec(memory_space=pltpu.VMEM)] * count
        + [pl.BlockSpec(memory_space=pl.ANY)] * len(earlier),
        out_specs=[pl.BlockSpec(memory_space=pltpu.VMEM)] * len(shapes),
        compiler_params=pltpu.CompilerParams(vmem_limit_bytes=VMEM_LIMIT),
        cost_estimate=pl.CostEstimate(flops=1, bytes_accessed=1, transcendentals=0),
    )(place, *operands, *earlier)


def position(y, c, u, t):
    step = 1 - 2 * c
    twin = jnp.where(t // 2 == c, 0, 1)
    slot = ((y - u) * step * (1 - 2 * twin) + 16) % 4
    return twin * 8 + slot * 2 + t % 2


def stage_kernel(place, *refs):
    count = len(refs) // 2
    for i in range(count):
        refs[count + i][...] = refs[i][...]


def weights_kernel(place, gate, up, down, both, same):
    units = gate.shape[1]
    both[:, :units], both[:, units:] = gate[...], up[...]
    same[...] = down[...]


def tiles(size, tile=256):
    return [slice(i, min(i + tile, size)) for i in range(0, size, tile)]


def forward_kernel(half, place, panel_in, panel_cot, both, down, *outs):
    units = down.shape[0]
    start = half * panel_in.shape[0] // 2
    for left, weight, product, wide in (
        (panel_in, both, lambda a, t: jnp.dot(a, both[:, t], preferred_element_type=F32), 2 * units),
        (panel_cot, down, lambda a, t: contract_cols(a, down[t]), units),
    ):
        chunks = [o for o in outs if o.shape[1] == wide]
        rows = chunks[0].shape[0]
        for t in tiles(wide):
            whole = product(left[pl.ds(start, rows * len(chunks))], t).astype(BF16)
            for i, chunk in enumerate(chunks):
                chunk[:, t] = whole[i * rows : (i + 1) * rows]


def to_input_kernel(place, whole, both, *refs):
    part = refs[-2] if len(refs) > 1 else refs[-1]
    for t in tiles(both.shape[0]):
        part[:, t] = contract_cols(whole[...], both[t]).astype(BF16)
    if len(refs) > 1:
        refs[-1][...] = refs[0][...]


def line_up_kernel(first, n, place, *refs):
    blocks, (line_in, line_cot) = refs[:8], refs[8:]
    rows = pl.ds(first, n)
    for m in range(4):
        line_in[m] = blocks[m][rows]
        line_cot[m] = blocks[4 + m][rows]


def panels_kernel(place, *refs):
    y, c = place[0], place[1]
    step = 1 - 2 * c
    blocks, (panel_in, panel_cot) = refs[:8], refs[8:]
    for k in range(4):
        for m in range(4):
            far, near = (step * k + 4) % 4, (step * m + 4) % 4
            panel_in[position(y, c, far, near)] = blocks[k][m]
            panel_cot[position(y, c, near, far)] = blocks[4 + k][m]


def halves_kernel(place, own_both, own_down, *refs):
    twin_both = [r for r in refs[:-2] if r.shape[1] == own_both.shape[1]]
    twin_down = [r for r in refs[:-2] if r.shape[1] == own_down.shape[1]]
    first, rest = refs[-2:]
    rows, units = first.shape[1:]
    for j in range(4):
        part = pl.ds(j * rows, rows)
        for i in range(3):
            own, twins = (own_both, twin_both) if i < 2 else (own_down, twin_down)
            columns = slice(i * units, (i + 1) * units) if i < 2 else slice(None)
            per = 4 // len(twins)
            there = pl.ds(j % per * rows, rows)
            a, b = own[part, columns], twins[j // per][there, columns]
            total = (a.astype(F32) + b.astype(F32)).astype(BF16)
            if j == 1:
                first[i] = total
            else:
                rest[(j + 2) % 4, i] = total


def add_kernel(j, place, received, rest, total):
    total[...] = (received[...].astype(F32) + rest[j].astype(F32)).astype(BF16)


def grads_kernel(place, received, rest, *refs):
    gate_up, hidden = refs[-2:]
    gate_sum = received[0].astype(F32) + rest[2, 0].astype(F32)
    up_sum = received[1].astype(F32) + rest[2, 1].astype(F32)
    hidden_grad = received[2].astype(F32) + rest[2, 2].astype(F32)
    s = 1.0 / (1.0 + jnp.exp(-gate_sum))
    silu = gate_sum * s
    gate_up[0] = (hidden_grad * up_sum * s * (1.0 + gate_sum * (1.0 - s))).astype(BF16)
    gate_up[1] = (hidden_grad * silu).astype(BF16)
    if len(refs) == 3:
        start = refs[0].shape[0]
        hidden[:start] = refs[0][...]
        hidden[start:] = (silu * up_sum).astype(BF16)
    else:
        hidden[...] = (silu * up_sum).astype(BF16)


def pair_kernel(place, *refs):
    blocks, whole = refs[:8], refs[8]
    rows, units = blocks[0].shape[1:]
    for j in range(8):
        part = pl.ds(j * rows, rows)
        whole[part, :units] = blocks[j][0]
        whole[part, units:] = blocks[j][1]


def split_kernel(place, *refs):
    blocks, wholes = refs[:8], refs[8:]
    start = 0
    for whole in wholes:
        rows = whole.shape[0] // 8
        for j in range(8):
            whole[pl.ds(j * rows, rows)] = blocks[j][pl.ds(start, rows)]
        start += rows


def by_target_kernel(place, part_0, part_1, mine, left, right, far_up, far_down):
    y, c = place[0], place[1]
    mid = part_0.shape[-1] // 2
    for a in range(4):
        for b in range(4):
            at = position(y, c, jnp.where(c == 0, b, a), jnp.where(c == 0, a, b))
            for part, rows in ((part_0, slice(0, SPLIT)), (part_1, slice(SPLIT, None))):
                block = part[at]
                if a == 2:
                    far_up[b, rows] = block[:, :mid]
                    far_down[b, rows] = block[:, mid:]
                else:
                    (mine, left, None, right)[a][b, rows] = block


def relay_kernel(place, left, right, up, down, to_left, to_right):
    mid = left.shape[-1] // 2
    to_left[:, :, :mid] = left[:, :, :mid]
    to_left[:, :, mid:] = (left[:, :, mid:].astype(F32) + down[...].astype(F32)).astype(BF16)
    to_right[:, :, :mid] = (right[:, :, :mid].astype(F32) + up[...].astype(F32)).astype(BF16)
    to_right[:, :, mid:] = right[:, :, mid:]


def line_kernel(place, mine, from_left, from_right, own, *others):
    for k in range(4):
        total = mine[k].astype(F32) + from_left[k].astype(F32) + from_right[k].astype(F32)
        if k == 0:
            own[...] = total
        else:
            others[k - 1][...] = total.astype(BF16)


def sum_kernel(place, own, one, two, three, out):
    total = own[...] + one[...].astype(F32) + two[...].astype(F32) + three[...].astype(F32)
    out[...] = total.astype(BF16)


def local(tokens, cotangent, gate_weight, up_weight, down_weight):
    row, col = lax.axis_index("row"), lax.axis_index("col")
    place = jnp.stack([row // 2, row % 2]).astype(jnp.int32)
    length, width = tokens.shape
    units = gate_weight.shape[1]
    mid = width // 2
    sizes = (SPLIT, length - SPLIT)

    n0, n1 = sizes
    earlier = []

    def arrive(*values):
        earlier.extend(values)
        return list(values)

    def run(kernel, shapes, *values):
        known = {id(v) for v in values}
        out = local_call(kernel, shapes, place, values, [v for v in earlier if id(v) not in known])
        earlier[:] = out[:1]
        return out

    def first(pair):
        return [send(pair[0], ALONG_Z), send(pair[1], ALONG_X)]

    def second(pair):
        return [send(pair[0], ALONG_X), send(pair[1], ALONG_Z)]

    def up_y(value):
        return send(value, ALONG_Y)

    def twin(value):
        return send(value, TO_TWIN)

    near = [[tokens, cotangent]]
    p = first(near[0])
    near[0] = run(stage_kernel, [tokens.shape] * 2, *near[0])
    for hop in range(3):
        near.append(arrive(*p))
        if hop < 2:
            p = first(near[-1])
    shards = [near[m][i] for i in range(2) for m in range(4)]

    def line_up(start, n):
        kernel = functools.partial(line_up_kernel, start, n)
        return run(kernel, [(4, n, width)] * 2, *shards)

    l0 = [line_up(0, n0)]
    s0 = second(l0[0])
    l1 = [line_up(n0, n1)]
    s1 = second(l1[0])
    weights = [gate_weight, up_weight, down_weight]
    both_weight, down_weight = run(weights_kernel, [(width, 2 * units), down_weight.shape], *weights
    )
    for hop in range(2):
        l0.append(arrive(*s0))
        s0 = second(l0[-1])
        l1.append(arrive(*s1))
        s1 = second(l1[-1])
    l0.append(arrive(*s0))

    def panels(n, lines):
        blocks = [lines[k][i] for i in range(2) for k in range(4)]
        both = run(panels_kernel, [(16, n, width)] * 2, *blocks)
        return [p.reshape(16 * n, width) for p in both]

    def forward(n, half, panel_in, panel_cot):
        kernel = functools.partial(forward_kernel, half)
        pieces = (GATE_UP_PIECES, BACK_PIECES) if half else (1, 1)
        shapes = [(8 * n // pieces[0], 2 * units)] * pieces[0]
        shapes += [(8 * n // pieces[1], units)] * pieces[1]
        return run(kernel, shapes, panel_in, panel_cot, both_weight, down_weight)

    def halves(n, own, theirs):
        shape = (3, 2 * n, units)
        return run(halves_kernel, [shape, (3,) + shape], *own, *theirs)

    def add(j, received, rest):
        kernel = functools.partial(add_kernel, j)
        return run(kernel, [received.shape], received, rest)[0]

    def grads(n, received, rest, *before):
        rows = 2 * n + sum(v.shape[0] for v in before)
        shapes = [(2, 2 * n, units), (rows, units)]
        return run(grads_kernel, shapes, received, rest, *before)

    def pair(n, blocks, twins):
        return run(pair_kernel, [(16 * n, 2 * units)], *blocks, *twins)[0]

    def pass_on(sent, held, held_twin, more=True):
        held.extend(arrive(sent))
        if more:
            sent = up_y(held[-1])
        held_twin.append(twin(held[-1]))
        return sent

    in0, cot0 = panels(n0, l0)
    theirs0 = [twin(v) for v in forward(n0, 1, in0, cot0)]
    own0 = forward(n0, 0, in0, cot0)
    l1.append(arrive(*s1))
    first0, rest0 = halves(n0, own0, theirs0)
    r0 = up_y(first0)
    in1, cot1 = panels(n1, l1)
    theirs1 = [twin(v) for v in forward(n1, 1, in1, cot1)]
    r0 = up_y(add(0, r0, rest0))
    own1 = forward(n1, 0, in1, cot1)
    first1, rest1 = halves(n1, own1, theirs1)
    r1 = up_y(first1)
    r0 = up_y(add(1, r0, rest0))
    r1 = up_y(add(0, r1, rest1))
    gu0, hid = grads(n0, r0, rest0)
    g = up_y(gu0)
    g0, g0_twin = [gu0], [twin(gu0)]
    r1 = up_y(add(1, r1, rest1))
    g = pass_on(g, g0, g0_twin)
    gu1, hid = grads(n1, r1, rest1, hid)
    q = up_y(gu1)
    g1, g1_twin, h0, h0_twin = [gu1], [twin(gu1)], [], []
    g = pass_on(g, g0, g0_twin)
    q = pass_on(q, g1, g1_twin)
    pass_on(g, g0, g0_twin, False)
    q = pass_on(q, g1, g1_twin)
    whole0 = pair(n0, g0, g0_twin)
    part0, hid = run(to_input_kernel, [(16 * n0, width), hid.shape], whole0, both_weight, hid)
    h = up_y(hid)
    h0, h0_twin = [hid], [twin(hid)]
    pass_on(q, g1, g1_twin, False)
    whole1 = pair(n1, g1, g1_twin)
    (part1,) = run(to_input_kernel, [(16 * n1, width)], whole1, both_weight)
    wide, slim = (4, length, width), (4, length, mid)
    mine, left, right, far_up, far_down = run(
        by_target_kernel,
        [wide, wide, wide, slim, slim],
        part0.reshape(16, n0, width),
        part1.reshape(16, n1, width),
    )
    far_up, far_down = send(far_up, first_axis(1)), send(far_down, first_axis(-1))
    left, right = run(relay_kernel, [wide, wide], left, right, far_up, far_down)
    from_left, from_right = send(right, first_axis(1)), send(left, first_axis(-1))
    h = pass_on(h, h0, h0_twin)
    h = pass_on(h, h0, h0_twin)
    pass_on(h, h0, h0_twin, False)
    hid0, hid1 = run(split_kernel, [(16 * n, units) for n in sizes], *h0, *h0_twin)
    line_shapes = [jax.ShapeDtypeStruct(tokens.shape, F32)] + [tokens.shape] * 3
    line = run(line_kernel, line_shapes, mine, from_left, from_right)
    line = [line[0]] + [send(line[k], second_axis(-k)) for k in (1, 2, 3)]
    (grad_input,) = run(sum_kernel, [tokens.shape], *line)
    grad_gate = contract_rows(in0, whole0[:, :units]) + contract_rows(in1, whole1[:, :units])
    grad_up = contract_rows(in0, whole0[:, units:]) + contract_rows(in1, whole1[:, units:])
    grad_down = contract_rows(hid0, cot0) + contract_rows(hid1, cot1)
    return (grad_input, grad_gate, grad_up, grad_down)


def solution(mesh):
    return jax.shard_map(
        local,
        mesh=mesh,
        in_specs=(
            P("col", "row"),
            P("col", "row"),
            P("row", "col"),
            P("row", "col"),
            P("col", "row"),
        ),
        out_specs=(P("col", "row"), P("row", "col"), P("row", "col"), P("col", "row")),
        check_vma=False,
    )
```

```python
import functools

import jax
import jax.numpy as jnp
from jax import lax
from jax.experimental import pallas as pl
from jax.experimental.pallas import tpu as pltpu
from jax.sharding import PartitionSpec as P

BF16 = jnp.bfloat16
F32 = jnp.float32
GATE_UP_PIECES = 4
BACK_PIECES = 4
SPLIT = 64
AXES = ("row", "col")
VMEM_LIMIT = 24 * 2**20


def device(y, core, x, z):
    return (((y % 4) * 2 + core) * 4 + x % 4) * 4 + z % 4


def pairs(move):
    return [
        (device(y, c, x, z), device(*move(y, c, x, z)))
        for y in range(4)
        for c in range(2)
        for x in range(4)
        for z in range(4)
    ]


def sign(c):
    return 1 - 2 * c


ALONG_X = pairs(lambda y, c, x, z: (y, c, x + sign(c), z))
ALONG_Y = pairs(lambda y, c, x, z: (y + sign(c), c, x, z))
ALONG_Z = pairs(lambda y, c, x, z: (y, c, x, z + sign(c)))
TO_TWIN = pairs(lambda y, c, x, z: (y, 1 - c, x, z))


def first_axis(k):
    return pairs(lambda y, c, x, z: (y, c, x, z + k) if c == 0 else (y, c, x + k, z))


def second_axis(k):
    return pairs(lambda y, c, x, z: (y, c, x + k, z) if c == 0 else (y, c, x, z + k))


def send(value, perm):
    return lax.ppermute(value, AXES, perm)


def contract_rows(left, right):
    return lax.dot_general(
        left, right, (((0,), (0,)), ((), ())), preferred_element_type=F32
    )


def contract_cols(left, right):
    return lax.dot_general(
        left, right, (((1,), (1,)), ((), ())), preferred_element_type=F32
    )


def local_call(kernel, out_shapes, place, operands, earlier):
    count = len(operands)

    def ordered(place_ref, *refs):
        kernel(place_ref, *refs[:count], *refs[count + len(earlier) :])

    shapes = [s if hasattr(s, "dtype") else jax.ShapeDtypeStruct(s, BF16) for s in out_shapes]
    return pl.pallas_call(
        ordered,
        out_shape=shapes,
        in_specs=[pl.BlockSpec(memory_space=pltpu.SMEM)]
        + [pl.BlockSpec(memory_space=pltpu.VMEM)] * count
        + [pl.BlockSpec(memory_space=pl.ANY)] * len(earlier),
        out_specs=[pl.BlockSpec(memory_space=pltpu.VMEM)] * len(shapes),
        compiler_params=pltpu.CompilerParams(vmem_limit_bytes=VMEM_LIMIT),
        cost_estimate=pl.CostEstimate(flops=1, bytes_accessed=1, transcendentals=0),
    )(place, *operands, *earlier)


def position(y, c, u, t):
    step = 1 - 2 * c
    twin = jnp.where(t // 2 == c, 0, 1)
    slot = ((y - u) * step * (1 - 2 * twin) + 16) % 4
    return twin * 8 + slot * 2 + t % 2


def stage_kernel(place, *refs):
    count = len(refs) // 2
    for i in range(count):
        refs[count + i][...] = refs[i][...]


def weights_kernel(place, gate, up, down, both, same):
    units = gate.shape[1]
    both[:, :units], both[:, units:] = gate[...], up[...]
    same[...] = down[...]


def tiles(size, tile=256):
    return [slice(i, min(i + tile, size)) for i in range(0, size, tile)]


def forward_kernel(half, place, panel_in, panel_cot, both, down, *outs):
    units = down.shape[0]
    start = half * panel_in.shape[0] // 2
    for left, weight, product, wide in (
        (panel_in, both, lambda a, t: jnp.dot(a, both[:, t], preferred_element_type=F32), 2 * units),
        (panel_cot, down, lambda a, t: contract_cols(a, down[t]), units),
    ):
        chunks = [o for o in outs if o.shape[1] == wide]
        rows = chunks[0].shape[0]
        for t in tiles(wide):
            whole = product(left[pl.ds(start, rows * len(chunks))], t).astype(BF16)
            for i, chunk in enumerate(chunks):
                chunk[:, t] = whole[i * rows : (i + 1) * rows]


def to_input_kernel(place, whole, both, *refs):
    part = refs[-2] if len(refs) > 1 else refs[-1]
    for t in tiles(both.shape[0]):
        part[:, t] = contract_cols(whole[...], both[t]).astype(BF16)
    if len(refs) > 1:
        refs[-1][...] = refs[0][...]


def line_up_kernel(first, n, place, *refs):
    blocks, (line_in, line_cot) = refs[:8], refs[8:]
    rows = pl.ds(first, n)
    for m in range(4):
        line_in[m] = blocks[m][rows]
        line_cot[m] = blocks[4 + m][rows]


def panels_kernel(place, *refs):
    y, c = place[0], place[1]
    step = 1 - 2 * c
    blocks, (panel_in, panel_cot) = refs[:8], refs[8:]
    for k in range(4):
        for m in range(4):
            far, near = (step * k + 4) % 4, (step * m + 4) % 4
            panel_in[position(y, c, far, near)] = blocks[k][m]
            panel_cot[position(y, c, near, far)] = blocks[4 + k][m]


def halves_kernel(place, own_both, own_down, *refs):
    twin_both = [r for r in refs[:-2] if r.shape[1] == own_both.shape[1]]
    twin_down = [r for r in refs[:-2] if r.shape[1] == own_down.shape[1]]
    first, rest = refs[-2:]
    rows, units = first.shape[1:]
    for j in range(4):
        part = pl.ds(j * rows, rows)
        for i in range(3):
            own, twins = (own_both, twin_both) if i < 2 else (own_down, twin_down)
            columns = slice(i * units, (i + 1) * units) if i < 2 else slice(None)
            per = 4 // len(twins)
            there = pl.ds(j % per * rows, rows)
            a, b = own[part, columns], twins[j // per][there, columns]
            total = (a.astype(F32) + b.astype(F32)).astype(BF16)
            if j == 1:
                first[i] = total
            else:
                rest[(j + 2) % 4, i] = total


def add_kernel(j, place, received, rest, total):
    total[...] = (received[...].astype(F32) + rest[j].astype(F32)).astype(BF16)


def grads_kernel(place, received, rest, *refs):
    gate_up, hidden = refs[-2:]
    gate_sum = received[0].astype(F32) + rest[2, 0].astype(F32)
    up_sum = received[1].astype(F32) + rest[2, 1].astype(F32)
    hidden_grad = received[2].astype(F32) + rest[2, 2].astype(F32)
    s = 1.0 / (1.0 + jnp.exp(-gate_sum))
    silu = gate_sum * s
    gate_up[0] = (hidden_grad * up_sum * s * (1.0 + gate_sum * (1.0 - s))).astype(BF16)
    gate_up[1] = (hidden_grad * silu).astype(BF16)
    if len(refs) == 3:
        start = refs[0].shape[0]
        hidden[:start] = refs[0][...]
        hidden[start:] = (silu * up_sum).astype(BF16)
    else:
        hidden[...] = (silu * up_sum).astype(BF16)


def pair_kernel(place, *refs):
    blocks, whole = refs[:8], refs[8]
    rows, units = blocks[0].shape[1:]
    for j in range(8):
        part = pl.ds(j * rows, rows)
        whole[part, :units] = blocks[j][0]
        whole[part, units:] = blocks[j][1]


def split_kernel(place, *refs):
    blocks, wholes = refs[:8], refs[8:]
    start = 0
    for whole in wholes:
        rows = whole.shape[0] // 8
        for j in range(8):
            whole[pl.ds(j * rows, rows)] = blocks[j][pl.ds(start, rows)]
        start += rows


def by_target_kernel(place, part_0, part_1, mine, left, right, far_up, far_down):
    y, c = place[0], place[1]
    mid = part_0.shape[-1] // 2
    for a in range(4):
        for b in range(4):
            at = position(y, c, jnp.where(c == 0, b, a), jnp.where(c == 0, a, b))
            for part, rows in ((part_0, slice(0, SPLIT)), (part_1, slice(SPLIT, None))):
                block = part[at]
                if a == 2:
                    far_up[b, rows] = block[:, :mid]
                    far_down[b, rows] = block[:, mid:]
                else:
                    (mine, left, None, right)[a][b, rows] = block


def relay_kernel(place, left, right, up, down, to_left, to_right):
    mid = left.shape[-1] // 2
    to_left[:, :, :mid] = left[:, :, :mid]
    to_left[:, :, mid:] = (left[:, :, mid:].astype(F32) + down[...].astype(F32)).astype(BF16)
    to_right[:, :, :mid] = (right[:, :, :mid].astype(F32) + up[...].astype(F32)).astype(BF16)
    to_right[:, :, mid:] = right[:, :, mid:]


def line_kernel(place, mine, from_left, from_right, own, *others):
    for k in range(4):
        total = mine[k].astype(F32) + from_left[k].astype(F32) + from_right[k].astype(F32)
        if k == 0:
            own[...] = total
        else:
            others[k - 1][...] = total.astype(BF16)


def sum_kernel(place, own, one, two, three, out):
    total = own[...] + one[...].astype(F32) + two[...].astype(F32) + three[...].astype(F32)
    out[...] = total.astype(BF16)


def local(tokens, cotangent, gate_weight, up_weight, down_weight):
    row, col = lax.axis_index("row"), lax.axis_index("col")
    place = jnp.stack([row // 2, row % 2]).astype(jnp.int32)
    length, width = tokens.shape
    units = gate_weight.shape[1]
    mid = width // 2
    sizes = (SPLIT, length - SPLIT)

    n0, n1 = sizes
    earlier = []

    def arrive(*values):
        earlier.extend(values)
        return list(values)

    def run(kernel, shapes, *values):
        known = {id(v) for v in values}
        out = local_call(kernel, shapes, place, values, [v for v in earlier if id(v) not in known])
        earlier[:] = out[:1]
        return out

    def first(pair):
        return [send(pair[0], ALONG_Z), send(pair[1], ALONG_X)]

    def second(pair):
        return [send(pair[0], ALONG_X), send(pair[1], ALONG_Z)]

    def up_y(value):
        return send(value, ALONG_Y)

    def twin(value):
        return send(value, TO_TWIN)

    near = [[tokens, cotangent]]
    p = first(near[0])
    near[0] = run(stage_kernel, [tokens.shape] * 2, *near[0])
    for hop in range(3):
        near.append(arrive(*p))
        if hop < 2:
            p = first(near[-1])
    shards = [near[m][i] for i in range(2) for m in range(4)]

    def line_up(start, n):
        kernel = functools.partial(line_up_kernel, start, n)
        return run(kernel, [(4, n, width)] * 2, *shards)

    l0 = [line_up(0, n0)]
    s0 = second(l0[0])
    l1 = [line_up(n0, n1)]
    s1 = second(l1[0])
    weights = [gate_weight, up_weight, down_weight]
    both_weight, down_weight = run(weights_kernel, [(width, 2 * units), down_weight.shape], *weights
    )
    for hop in range(2):
        l0.append(arrive(*s0))
        s0 = second(l0[-1])
        l1.append(arrive(*s1))
        s1 = second(l1[-1])
    l0.append(arrive(*s0))

    def panels(n, lines):
        blocks = [lines[k][i] for i in range(2) for k in range(4)]
        both = run(panels_kernel, [(16, n, width)] * 2, *blocks)
        return [p.reshape(16 * n, width) for p in both]

    def forward(n, half, panel_in, panel_cot):
        kernel = functools.partial(forward_kernel, half)
        pieces = (GATE_UP_PIECES, BACK_PIECES) if half else (1, 1)
        shapes = [(8 * n // pieces[0], 2 * units)] * pieces[0]
        shapes += [(8 * n // pieces[1], units)] * pieces[1]
        return run(kernel, shapes, panel_in, panel_cot, both_weight, down_weight)

    def halves(n, own, theirs):
        shape = (3, 2 * n, units)
        return run(halves_kernel, [shape, (3,) + shape], *own, *theirs)

    def add(j, received, rest):
        kernel = functools.partial(add_kernel, j)
        return run(kernel, [received.shape], received, rest)[0]

    def grads(n, received, rest, *before):
        rows = 2 * n + sum(v.shape[0] for v in before)
        shapes = [(2, 2 * n, units), (rows, units)]
        return run(grads_kernel, shapes, received, rest, *before)

    def pair(n, blocks, twins):
        return run(pair_kernel, [(16 * n, 2 * units)], *blocks, *twins)[0]

    def pass_on(sent, held, held_twin, more=True):
        held.extend(arrive(sent))
        if more:
            sent = up_y(held[-1])
        held_twin.append(twin(held[-1]))
        return sent

    in0, cot0 = panels(n0, l0)
    theirs0 = [twin(v) for v in forward(n0, 1, in0, cot0)]
    own0 = forward(n0, 0, in0, cot0)
    l1.append(arrive(*s1))
    first0, rest0 = halves(n0, own0, theirs0)
    r0 = up_y(first0)
    in1, cot1 = panels(n1, l1)
    theirs1 = [twin(v) for v in forward(n1, 1, in1, cot1)]
    r0 = up_y(add(0, r0, rest0))
    own1 = forward(n1, 0, in1, cot1)
    first1, rest1 = halves(n1, own1, theirs1)
    r1 = up_y(first1)
    r0 = up_y(add(1, r0, rest0))
    r1 = up_y(add(0, r1, rest1))
    gu0, hid = grads(n0, r0, rest0)
    g = up_y(gu0)
    g0, g0_twin = [gu0], [twin(gu0)]
    r1 = up_y(add(1, r1, rest1))
    gu1, hid = grads(n1, r1, rest1, hid)
    g = pass_on(g, g0, g0_twin)
    q = up_y(gu1)
    g1, g1_twin, h0, h0_twin = [gu1], [twin(gu1)], [], []
    g = pass_on(g, g0, g0_twin)
    q = pass_on(q, g1, g1_twin)
    pass_on(g, g0, g0_twin, False)
    q = pass_on(q, g1, g1_twin)
    whole0 = pair(n0, g0, g0_twin)
    part0, hid = run(to_input_kernel, [(16 * n0, width), hid.shape], whole0, both_weight, hid)
    h = up_y(hid)
    h0, h0_twin = [hid], [twin(hid)]
    pass_on(q, g1, g1_twin, False)
    whole1 = pair(n1, g1, g1_twin)
    (part1,) = run(to_input_kernel, [(16 * n1, width)], whole1, both_weight)
    wide, slim = (4, length, width), (4, length, mid)
    mine, left, right, far_up, far_down = run(
        by_target_kernel,
        [wide, wide, wide, slim, slim],
        part0.reshape(16, n0, width),
        part1.reshape(16, n1, width),
    )
    far_up, far_down = send(far_up, first_axis(1)), send(far_down, first_axis(-1))
    left, right = run(relay_kernel, [wide, wide], left, right, far_up, far_down)
    from_left, from_right = send(right, first_axis(1)), send(left, first_axis(-1))
    h = pass_on(h, h0, h0_twin)
    h = pass_on(h, h0, h0_twin)
    pass_on(h, h0, h0_twin, False)
    hid0, hid1 = run(split_kernel, [(16 * n, units) for n in sizes], *h0, *h0_twin)
    line_shapes = [jax.ShapeDtypeStruct(tokens.shape, F32)] + [tokens.shape] * 3
    line = run(line_kernel, line_shapes, mine, from_left, from_right)
    line = [line[0]] + [send(line[k], second_axis(-k)) for k in (1, 2, 3)]
    (grad_input,) = run(sum_kernel, [tokens.shape], *line)
    grad_gate = contract_rows(in0, whole0[:, :units]) + contract_rows(in1, whole1[:, :units])
    grad_up = contract_rows(in0, whole0[:, units:]) + contract_rows(in1, whole1[:, units:])
    grad_down = contract_rows(hid0, cot0) + contract_rows(hid1, cot1)
    return (grad_input, grad_gate, grad_up, grad_down)


def solution(mesh):
    return jax.shard_map(
        local,
        mesh=mesh,
        in_specs=(
            P("col", "row"),
            P("col", "row"),
            P("row", "col"),
            P("row", "col"),
            P("col", "row"),
        ),
        out_specs=(P("col", "row"), P("row", "col"), P("row", "col"), P("col", "row")),
        check_vma=False,
    )
```

```python
import functools

import jax
import jax.numpy as jnp
from jax import lax
from jax.experimental import pallas as pl
from jax.experimental.pallas import tpu as pltpu
from jax.sharding import PartitionSpec as P

BF16 = jnp.bfloat16
F32 = jnp.float32
GATE_UP_PIECES = 4
BACK_PIECES = 4
SPLIT = 64
AXES = ("row", "col")
VMEM_LIMIT = 24 * 2**20


def device(y, core, x, z):
    return (((y % 4) * 2 + core) * 4 + x % 4) * 4 + z % 4


def pairs(move):
    return [
        (device(y, c, x, z), device(*move(y, c, x, z)))
        for y in range(4)
        for c in range(2)
        for x in range(4)
        for z in range(4)
    ]


def sign(c):
    return 1 - 2 * c


ALONG_X = pairs(lambda y, c, x, z: (y, c, x + sign(c), z))
ALONG_Y = pairs(lambda y, c, x, z: (y + sign(c), c, x, z))
ALONG_Z = pairs(lambda y, c, x, z: (y, c, x, z + sign(c)))
TO_TWIN = pairs(lambda y, c, x, z: (y, 1 - c, x, z))


def first_axis(k):
    return pairs(lambda y, c, x, z: (y, c, x, z + k) if c == 0 else (y, c, x + k, z))


def second_axis(k):
    return pairs(lambda y, c, x, z: (y, c, x + k, z) if c == 0 else (y, c, x, z + k))


def send(value, perm):
    return lax.ppermute(value, AXES, perm)


def contract_rows(left, right):
    return lax.dot_general(
        left, right, (((0,), (0,)), ((), ())), preferred_element_type=F32
    )


def contract_cols(left, right):
    return lax.dot_general(
        left, right, (((1,), (1,)), ((), ())), preferred_element_type=F32
    )


def local_call(kernel, out_shapes, place, operands, earlier):
    count = len(operands)

    def ordered(place_ref, *refs):
        kernel(place_ref, *refs[:count], *refs[count + len(earlier) :])

    shapes = [s if hasattr(s, "dtype") else jax.ShapeDtypeStruct(s, BF16) for s in out_shapes]
    return pl.pallas_call(
        ordered,
        out_shape=shapes,
        in_specs=[pl.BlockSpec(memory_space=pltpu.SMEM)]
        + [pl.BlockSpec(memory_space=pltpu.VMEM)] * count
        + [pl.BlockSpec(memory_space=pl.ANY)] * len(earlier),
        out_specs=[pl.BlockSpec(memory_space=pltpu.VMEM)] * len(shapes),
        compiler_params=pltpu.CompilerParams(vmem_limit_bytes=VMEM_LIMIT),
        cost_estimate=pl.CostEstimate(flops=1, bytes_accessed=1, transcendentals=0),
    )(place, *operands, *earlier)


def position(y, c, u, t):
    step = 1 - 2 * c
    twin = jnp.where(t // 2 == c, 0, 1)
    slot = ((y - u) * step * (1 - 2 * twin) + 16) % 4
    return twin * 8 + slot * 2 + t % 2


def stage_kernel(place, *refs):
    count = len(refs) // 2
    for i in range(count):
        refs[count + i][...] = refs[i][...]


def weights_kernel(place, gate, up, down, both, same):
    units = gate.shape[1]
    both[:, :units], both[:, units:] = gate[...], up[...]
    same[...] = down[...]


def tiles(size, tile=256):
    return [slice(i, min(i + tile, size)) for i in range(0, size, tile)]


def forward_kernel(half, place, panel_in, panel_cot, both, down, *outs):
    units = down.shape[0]
    start = half * panel_in.shape[0] // 2
    for left, weight, product, wide in (
        (panel_in, both, lambda a, t: jnp.dot(a, both[:, t], preferred_element_type=F32), 2 * units),
        (panel_cot, down, lambda a, t: contract_cols(a, down[t]), units),
    ):
        chunks = [o for o in outs if o.shape[1] == wide]
        rows = chunks[0].shape[0]
        for t in tiles(wide):
            whole = product(left[pl.ds(start, rows * len(chunks))], t).astype(BF16)
            for i, chunk in enumerate(chunks):
                chunk[:, t] = whole[i * rows : (i + 1) * rows]


def to_input_kernel(place, whole, both, *refs):
    part = refs[-2] if len(refs) > 1 else refs[-1]
    for t in tiles(both.shape[0]):
        part[:, t] = contract_cols(whole[...], both[t]).astype(BF16)
    if len(refs) > 1:
        refs[-1][...] = refs[0][...]


def line_up_kernel(first, n, place, *refs):
    blocks, (line_in, line_cot) = refs[:8], refs[8:]
    rows = pl.ds(first, n)
    for m in range(4):
        line_in[m] = blocks[m][rows]
        line_cot[m] = blocks[4 + m][rows]


def panels_kernel(place, *refs):
    y, c = place[0], place[1]
    step = 1 - 2 * c
    blocks, (panel_in, panel_cot) = refs[:8], refs[8:]
    for k in range(4):
        for m in range(4):
            far, near = (step * k + 4) % 4, (step * m + 4) % 4
            panel_in[position(y, c, far, near)] = blocks[k][m]
            panel_cot[position(y, c, near, far)] = blocks[4 + k][m]


def halves_kernel(place, own_both, own_down, *refs):
    twin_both = [r for r in refs[:-2] if r.shape[1] == own_both.shape[1]]
    twin_down = [r for r in refs[:-2] if r.shape[1] == own_down.shape[1]]
    first, rest = refs[-2:]
    rows, units = first.shape[1:]
    for j in range(4):
        part = pl.ds(j * rows, rows)
        for i in range(3):
            own, twins = (own_both, twin_both) if i < 2 else (own_down, twin_down)
            columns = slice(i * units, (i + 1) * units) if i < 2 else slice(None)
            per = 4 // len(twins)
            there = pl.ds(j % per * rows, rows)
            a, b = own[part, columns], twins[j // per][there, columns]
            total = (a.astype(F32) + b.astype(F32)).astype(BF16)
            if j == 1:
                first[i] = total
            else:
                rest[(j + 2) % 4, i] = total


def add_kernel(j, place, received, rest, total):
    total[...] = (received[...].astype(F32) + rest[j].astype(F32)).astype(BF16)


def grads_kernel(place, received, rest, *refs):
    gate_up, hidden = refs[-2:]
    gate_sum = received[0].astype(F32) + rest[2, 0].astype(F32)
    up_sum = received[1].astype(F32) + rest[2, 1].astype(F32)
    hidden_grad = received[2].astype(F32) + rest[2, 2].astype(F32)
    s = 1.0 / (1.0 + jnp.exp(-gate_sum))
    silu = gate_sum * s
    gate_up[0] = (hidden_grad * up_sum * s * (1.0 + gate_sum * (1.0 - s))).astype(BF16)
    gate_up[1] = (hidden_grad * silu).astype(BF16)
    if len(refs) == 3:
        start = refs[0].shape[0]
        hidden[:start] = refs[0][...]
        hidden[start:] = (silu * up_sum).astype(BF16)
    else:
        hidden[...] = (silu * up_sum).astype(BF16)


def pair_kernel(place, *refs):
    blocks, whole = refs[:8], refs[8]
    rows, units = blocks[0].shape[1:]
    for j in range(8):
        part = pl.ds(j * rows, rows)
        whole[part, :units] = blocks[j][0]
        whole[part, units:] = blocks[j][1]


def split_kernel(place, *refs):
    blocks, wholes = refs[:8], refs[8:]
    start = 0
    for whole in wholes:
        rows = whole.shape[0] // 8
        for j in range(8):
            whole[pl.ds(j * rows, rows)] = blocks[j][pl.ds(start, rows)]
        start += rows


def by_target_kernel(place, part_0, part_1, mine, left, right, far_up, far_down):
    y, c = place[0], place[1]
    mid = part_0.shape[-1] // 2
    for a in range(4):
        for b in range(4):
            at = position(y, c, jnp.where(c == 0, b, a), jnp.where(c == 0, a, b))
            for part, rows in ((part_0, slice(0, SPLIT)), (part_1, slice(SPLIT, None))):
                block = part[at]
                if a == 2:
                    far_up[b, rows] = block[:, :mid]
                    far_down[b, rows] = block[:, mid:]
                else:
                    (mine, left, None, right)[a][b, rows] = block


def relay_kernel(place, left, right, up, down, held, to_left, to_right, onward):
    onward[...] = held[...]
    mid = left.shape[-1] // 2
    to_left[:, :, :mid] = left[:, :, :mid]
    to_left[:, :, mid:] = (left[:, :, mid:].astype(F32) + down[...].astype(F32)).astype(BF16)
    to_right[:, :, :mid] = (right[:, :, :mid].astype(F32) + up[...].astype(F32)).astype(BF16)
    to_right[:, :, mid:] = right[:, :, mid:]


def line_kernel(place, mine, from_left, from_right, own, *others):
    for k in range(4):
        total = mine[k].astype(F32) + from_left[k].astype(F32) + from_right[k].astype(F32)
        if k == 0:
            own[...] = total
        else:
            others[k - 1][...] = total.astype(BF16)


def sum_kernel(place, own, one, two, three, out):
    total = own[...] + one[...].astype(F32) + two[...].astype(F32) + three[...].astype(F32)
    out[...] = total.astype(BF16)


def local(tokens, cotangent, gate_weight, up_weight, down_weight):
    row, col = lax.axis_index("row"), lax.axis_index("col")
    place = jnp.stack([row // 2, row % 2]).astype(jnp.int32)
    length, width = tokens.shape
    units = gate_weight.shape[1]
    mid = width // 2
    sizes = (SPLIT, length - SPLIT)

    n0, n1 = sizes
    earlier = []

    def arrive(*values):
        earlier.extend(values)
        return list(values)

    def run(kernel, shapes, *values):
        known = {id(v) for v in values}
        out = local_call(kernel, shapes, place, values, [v for v in earlier if id(v) not in known])
        earlier[:] = out[:1]
        return out

    def first(pair):
        return [send(pair[0], ALONG_Z), send(pair[1], ALONG_X)]

    def second(pair):
        return [send(pair[0], ALONG_X), send(pair[1], ALONG_Z)]

    def up_y(value):
        return send(value, ALONG_Y)

    def twin(value):
        return send(value, TO_TWIN)

    near = [[tokens, cotangent]]
    p = first(near[0])
    near[0] = run(stage_kernel, [tokens.shape] * 2, *near[0])
    for hop in range(3):
        near.append(arrive(*p))
        if hop < 2:
            p = first(near[-1])
    shards = [near[m][i] for i in range(2) for m in range(4)]

    def line_up(start, n):
        kernel = functools.partial(line_up_kernel, start, n)
        return run(kernel, [(4, n, width)] * 2, *shards)

    l0 = [line_up(0, n0)]
    s0 = second(l0[0])
    l1 = [line_up(n0, n1)]
    s1 = second(l1[0])
    weights = [gate_weight, up_weight, down_weight]
    both_weight, down_weight = run(weights_kernel, [(width, 2 * units), down_weight.shape], *weights
    )
    for hop in range(2):
        l0.append(arrive(*s0))
        s0 = second(l0[-1])
        l1.append(arrive(*s1))
        s1 = second(l1[-1])
    l0.append(arrive(*s0))

    def panels(n, lines):
        blocks = [lines[k][i] for i in range(2) for k in range(4)]
        both = run(panels_kernel, [(16, n, width)] * 2, *blocks)
        return [p.reshape(16 * n, width) for p in both]

    def forward(n, half, panel_in, panel_cot):
        kernel = functools.partial(forward_kernel, half)
        pieces = (GATE_UP_PIECES, BACK_PIECES) if half else (1, 1)
        shapes = [(8 * n // pieces[0], 2 * units)] * pieces[0]
        shapes += [(8 * n // pieces[1], units)] * pieces[1]
        return run(kernel, shapes, panel_in, panel_cot, both_weight, down_weight)

    def halves(n, own, theirs):
        shape = (3, 2 * n, units)
        return run(halves_kernel, [shape, (3,) + shape], *own, *theirs)

    def add(j, received, rest):
        kernel = functools.partial(add_kernel, j)
        return run(kernel, [received.shape], received, rest)[0]

    def grads(n, received, rest, *before):
        rows = 2 * n + sum(v.shape[0] for v in before)
        shapes = [(2, 2 * n, units), (rows, units)]
        return run(grads_kernel, shapes, received, rest, *before)

    def pair(n, blocks, twins):
        return run(pair_kernel, [(16 * n, 2 * units)], *blocks, *twins)[0]

    def pass_on(sent, held, held_twin, more=True):
        held.extend(arrive(sent))
        if more:
            sent = up_y(held[-1])
        held_twin.append(twin(held[-1]))
        return sent

    in0, cot0 = panels(n0, l0)
    theirs0 = [twin(v) for v in forward(n0, 1, in0, cot0)]
    own0 = forward(n0, 0, in0, cot0)
    l1.append(arrive(*s1))
    first0, rest0 = halves(n0, own0, theirs0)
    r0 = up_y(first0)
    in1, cot1 = panels(n1, l1)
    theirs1 = [twin(v) for v in forward(n1, 1, in1, cot1)]
    r0 = up_y(add(0, r0, rest0))
    own1 = forward(n1, 0, in1, cot1)
    first1, rest1 = halves(n1, own1, theirs1)
    r1 = up_y(first1)
    r0 = up_y(add(1, r0, rest0))
    r1 = up_y(add(0, r1, rest1))
    gu0, hid = grads(n0, r0, rest0)
    g = up_y(gu0)
    g0, g0_twin = [gu0], [twin(gu0)]
    r1 = up_y(add(1, r1, rest1))
    gu1, hid = grads(n1, r1, rest1, hid)
    g = pass_on(g, g0, g0_twin)
    q = up_y(gu1)
    g1, g1_twin, h0, h0_twin = [gu1], [twin(gu1)], [], []
    g = pass_on(g, g0, g0_twin)
    q = pass_on(q, g1, g1_twin)
    pass_on(g, g0, g0_twin, False)
    q = pass_on(q, g1, g1_twin)
    whole0 = pair(n0, g0, g0_twin)
    part0, hid = run(to_input_kernel, [(16 * n0, width), hid.shape], whole0, both_weight, hid)
    h = up_y(hid)
    h0, h0_twin = [hid], [twin(hid)]
    pass_on(q, g1, g1_twin, False)
    whole1 = pair(n1, g1, g1_twin)
    (part1,) = run(to_input_kernel, [(16 * n1, width)], whole1, both_weight)
    wide, slim = (4, length, width), (4, length, mid)
    mine, left, right, far_up, far_down = run(
        by_target_kernel,
        [wide, wide, wide, slim, slim],
        part0.reshape(16, n0, width),
        part1.reshape(16, n1, width),
    )
    far_up, far_down = send(far_up, first_axis(1)), send(far_down, first_axis(-1))
    h = pass_on(h, h0, h0_twin)
    left, right, h2 = run(relay_kernel, [wide, wide, hid.shape], left, right, far_up, far_down, h)
    from_left, from_right = send(right, first_axis(1)), send(left, first_axis(-1))
    h3 = up_y(h2)
    h0 += [h2, h3]
    h0_twin += [twin(v) for v in (h2, h3)]
    hid0, hid1 = run(split_kernel, [(16 * n, units) for n in sizes], *h0, *h0_twin)
    line_shapes = [jax.ShapeDtypeStruct(tokens.shape, F32)] + [tokens.shape] * 3
    line = run(line_kernel, line_shapes, mine, from_left, from_right)
    line = [line[0]] + [send(line[k], second_axis(-k)) for k in (1, 2, 3)]
    (grad_input,) = run(sum_kernel, [tokens.shape], *line)
    grad_gate = contract_rows(in0, whole0[:, :units]) + contract_rows(in1, whole1[:, :units])
    grad_up = contract_rows(in0, whole0[:, units:]) + contract_rows(in1, whole1[:, units:])
    grad_down = contract_rows(hid0, cot0) + contract_rows(hid1, cot1)
    return (grad_input, grad_gate, grad_up, grad_down)


def solution(mesh):
    return jax.shard_map(
        local,
        mesh=mesh,
        in_specs=(
            P("col", "row"),
            P("col", "row"),
            P("row", "col"),
            P("row", "col"),
            P("col", "row"),
        ),
        out_specs=(P("col", "row"), P("row", "col"), P("row", "col"), P("col", "row")),
        check_vma=False,
    )
```
